32 devices in a mesh: section: 2 (over y), dp: 16 (over z, x, core).
Axes of the slice: x: 2, y: 2, z: 4, core: 2. Of those that a mesh axis runs over, the one named last changes fastest.
Arguments:
- tokens: bfloat16 [32, 512, 512], P('dp', 'section'), may hold values from -6 to 6
- segments: int32 [32, 512], P('dp'), may hold values from 0 to 3, never falling along the last dimension, each value on 1 to 256 neighbouring positions
- qkv_weight: float32 [2, 512, 1536], P('section', 'dp'), may hold values from -0.25 to 0.25
- out_weight: float32 [2, 512, 512], P('section', 'dp'), may hold values from -2 to 2
- up_weight: float32 [2, 512, 2048], P('section', 'dp'), may hold values from -0.25 to 0.25
- down_weight: float32 [2, 2048, 512], P('section', 'dp'), may hold values from -0.125 to 0.125
- norm_gains: float32 [2, 2, 512], P('section', None, 'dp'), may hold values from 0.5 to 1.5
- norm_biases: float32 [2, 2, 512], P('section', None, 'dp'), may hold values from -2 to 2
- pre_weight: float32 [512, 32], P(('section', 'dp')), may hold values from -0.25 to 0.25
- post_weight: float32 [32, 512], P(None, ('section', 'dp')), may hold values from -3 to 3
- codebook: float32 [8192, 32], P(('section', 'dp')), may hold values from -6 to 6
- quant_gain: float32 [512], P(('section', 'dp')), may hold values from 0.5 to 1.5
- quant_bias: float32 [512], P(('section', 'dp')), may hold values from -2 to 2
Outputs:
- grad_tokens: float32 [32, 512, 512], P('dp', 'section')
- grad_qkv: float32 [2, 512, 1536], P('section', 'dp')
- grad_out: float32 [2, 512, 512], P('section', 'dp')
- grad_up: float32 [2, 512, 2048], P('section', 'dp')
- grad_down: float32 [2, 2048, 512], P('section', 'dp')
- grad_gains: float32 [2, 2, 512], P('section', None, 'dp')
- grad_biases: float32 [2, 2, 512], P('section', None, 'dp')
- grad_pre: float32 [512, 32], P(('section', 'dp'))
- grad_post: float32 [32, 512], P(None, ('section', 'dp'))
- grad_codebook: float32 [8192, 32], P(('section', 'dp'))
- grad_quant_gain: float32 [512], P(('section', 'dp'))
- grad_quant_bias: float32 [512], P(('section', 'dp'))
The draws below stay inside these ranges and needn't reach their ends.
Inputs may be any that keep to these rules, and one draw needn't show every extreme that they name: `segments`: along each row the ids never fall; each crop segment holds 1 to 256 tokens.
All inputs are finite; a program needn't handle non-finite values.
Results may differ from the reference program's by a relative error of at most 0.019.
Values may be sent and summed in bfloat16 or wider, within the bound.
A program may use at most 320 MiB of HBM per device.

```python
import math
from functools import partial
import jax
import jax.numpy as jnp
import numpy as np
from jax import lax

D = 512
HEADS = 8
HEAD_DIM = 64
FF = 2048
CODES = 8192
CODE_DIM = 32
LENGTH = 512
ROWS = 32
TOKENS = 16384


def levels(stream_key, extent, cuts, smallest, largest):
    gain, own = 1.0, jax.random.fold_in(stream_key, 6)
    for position, parts in cuts:
        draws = jnp.exp(jax.random.uniform(jax.random.fold_in(own, position), (parts,), jnp.float32, smallest / len(cuts), largest / len(cuts)))
        gain = gain * jnp.repeat(draws, extent[position] // parts).reshape([-1 if axis == position else 1 for axis in range(len(extent))])
    return gain


def profile(number_of, total, reach, lean):
    loads = [(1 << 20) // math.isqrt(rank ** lean) + 1 for rank in range(2, number_of + 1)]
    spare, holding = total - reach - (number_of - 1), [1] * (number_of - 1)
    while spare > 0:
        candidates = [i for i in range(number_of - 1) if holding[i] < reach]
        whole, left = sum([loads[i] for i in candidates]), spare
        for i in candidates:
            extra = min(reach - holding[i], max(1, left * loads[i] // whole), spare)
            holding[i] = holding[i] + extra
            spare = spare - extra
    return np.array([reach] + holding)


def ragged(own_key, number_of, total, limit, skew):
    if number_of == 2:
        one = jax.random.randint(own_key, (), max(1, total - limit), min(limit, total - 1) + 1)
        return jnp.stack([one, total - one])
    tallies = jnp.asarray(profile(number_of, total, limit, skew), jnp.int32)
    twos = (number_of - 1) // 2
    donor, receiver = tallies[1:1 + 2 * twos:2], tallies[2:2 + 2 * twos:2]
    margin = jnp.minimum(donor - 1, limit - receiver)
    moved = jax.random.randint(jax.random.fold_in(own_key, 1), (twos,), 0, 1 << 20) % (margin + 1)
    tallies = tallies.at[1:1 + 2 * twos:2].set(donor - moved).at[2:2 + 2 * twos:2].set(receiver + moved)
    return tallies[jax.random.permutation(jax.random.fold_in(own_key, 2), number_of)]


def normal_values(rng, shape, scale, most, pieces=(), dtype=jnp.bfloat16):
    gain = levels(rng, shape, pieces, -0.22, 0.18) if pieces else 1.0
    result = jax.random.normal(rng, shape, jnp.float32) * scale * gain
    return jnp.minimum(jnp.maximum(result, -most), most).astype(dtype)


def setup_inputs(seed: int = 0) -> dict:
    splits = jax.random.split(jax.random.key(seed), 14)
    tokens = normal_values(splits[0], (ROWS, LENGTH, D), 1.0, 6.0, ((0, 16), (1, 2)))
    segments = jax.vmap(lambda own: jnp.searchsorted(jnp.cumsum(ragged(own, 4, LENGTH, LENGTH // 2, 1)), jnp.arange(LENGTH), side="right"))(jax.random.split(splits[1], ROWS)).reshape((ROWS, LENGTH)).astype(jnp.int32)
    qkv_weight = normal_values(splits[2], (2, D, 3 * D), D ** -0.5, 0.25, ((0, 2), (1, 16)), jnp.float32)
    out_weight = normal_values(splits[3], (2, D, D), (D // 64) ** -0.5, 2.0, ((0, 2), (1, 16)), jnp.float32)
    up_weight = normal_values(splits[4], (2, D, FF), D ** -0.5, 0.25, ((0, 2), (1, 16)), jnp.float32)
    down_weight = normal_values(splits[5], (2, FF, D), FF ** -0.5, 0.125, ((0, 2), (1, 16)), jnp.float32)
    norm_gains = jnp.clip(1.0 + 0.1 * jax.random.normal(splits[6], (2, 2, D), jnp.float32), 0.5, 1.5)
    norm_biases = normal_values(splits[7], (2, 2, D), 0.3, 2.0, ((0, 2), (2, 16)), jnp.float32)
    pre_weight = normal_values(splits[8], (D, CODE_DIM), D ** -0.5, 0.25, ((0, 32),), jnp.float32)
    post_weight = normal_values(splits[9], (CODE_DIM, D), (CODE_DIM // 8) ** -0.5, 3.0, ((1, 32),), jnp.float32)
    codebook = normal_values(splits[10], (CODES, CODE_DIM), 1.0, 6.0, ((0, 32),), jnp.float32)
    quant_gain = jnp.clip(1.0 + 0.1 * jax.random.normal(splits[11], (D,), jnp.float32), 0.5, 1.5)
    quant_bias = normal_values(splits[12], (D,), 0.3, 2.0, ((0, 32),), jnp.float32)
    return dict(tokens=tokens, segments=segments, qkv_weight=qkv_weight, out_weight=out_weight, up_weight=up_weight, down_weight=down_weight, norm_gains=norm_gains, norm_biases=norm_biases, pre_weight=pre_weight, post_weight=post_weight, codebook=codebook, quant_gain=quant_gain, quant_bias=quant_bias)


EPS = 1e-05
BETA = 0.25
TEMP = 8.0
GELU_C = math.sqrt(2.0 / math.pi)
GELU_K = 0.044715
NEG_FILL = -1e+30
HIGH_PREC = lax.Precision.HIGHEST

@jax.custom_vjp
def low(v):
    return lax.optimization_barrier(v.astype(jnp.bfloat16)).astype(jnp.float32)

@jax.custom_vjp
def low_back(v):
    return v

def low_keep(v):
    return (low(v), None)

def low_pass(kept, grad):
    return (grad,)

def back_keep(v):
    return (v, None)

def back_low(kept, grad):
    return (low(grad),)
low.defvjp(low_keep, low_pass)
low_back.defvjp(back_keep, back_low)

def matmul_high(left, right):
    return jnp.dot(left, right, precision=HIGH_PREC, preferred_element_type=jnp.float32)

def layer_norm(values, gain_vec, bias_vec):
    center = lax.optimization_barrier(jnp.mean(values, axis=-1, keepdims=True))
    shifted = values - center
    return shifted * lax.rsqrt(lax.optimization_barrier(jnp.mean(shifted * shifted, axis=-1, keepdims=True)) + EPS) * gain_vec + bias_vec

def softmax_rows(scores):
    top_val = lax.optimization_barrier(jnp.max(scores, axis=-1, keepdims=True))
    expo_val = jnp.exp(scores - top_val)
    return expo_val / lax.optimization_barrier(jnp.sum(expo_val, axis=-1, keepdims=True))

def gelu_tanh(pre_act):
    return 0.5 * pre_act * (1.0 + jnp.tanh(GELU_C * (pre_act + GELU_K * pre_act * pre_act * pre_act)))

def block(rows_in, seg_row, w_qkv, w_out, w_up, w_down, gain_rows, bias_rows):
    attn_in = low(layer_norm(rows_in, gain_rows[0], bias_rows[0]))
    qkv_all = low(low_back(matmul_high(attn_in, w_qkv)))
    queries = qkv_all[:, :D].reshape(LENGTH, HEADS, HEAD_DIM)
    keys_all = qkv_all[:, D:2 * D].reshape(LENGTH, HEADS, HEAD_DIM)
    values_all = qkv_all[:, 2 * D:].reshape(LENGTH, HEADS, HEAD_DIM)
    scores = low_back(jnp.einsum('ihd,jhd->hij', queries, keys_all, precision=HIGH_PREC) * HEAD_DIM ** (-0.5))
    same_seg = seg_row[:, None] == seg_row[None, :]
    prob_vals = softmax_rows(jnp.where(same_seg[None], scores, NEG_FILL))
    mixed_out = jnp.einsum('hij,jhd->ihd', low(prob_vals), values_all, precision=HIGH_PREC).reshape(LENGTH, D)
    middle = rows_in + low_back(matmul_high(low(low_back(mixed_out)), w_out))
    mlp_in = low(layer_norm(middle, gain_rows[1], bias_rows[1]))
    hidden_act = low(gelu_tanh(low_back(matmul_high(mlp_in, w_up))))
    return middle + low_back(matmul_high(hidden_act, w_down))

def quantize(hidden_rows, qgain_low, qbias_low, pre_low, post_low, code_low):
    mapped = low(layer_norm(hidden_rows, qgain_low, qbias_low))
    raw_latent = low_back(matmul_high(mapped, pre_low))
    unit_latent = raw_latent * lax.rsqrt(lax.optimization_barrier(jnp.sum(raw_latent * raw_latent, axis=-1, keepdims=True)) + 1.0)
    logits = low_back(TEMP * matmul_high(low(unit_latent), code_low.T))
    quant_vals = low(low_back(matmul_high(low(softmax_rows(logits)), code_low)))
    gap_vals = unit_latent - quant_vals
    commit = jnp.sum(gap_vals * gap_vals)
    start_rows = low(low_back(matmul_high(quant_vals, post_low)))
    return (start_rows, commit)

def forward(segments, tokens_f, qkv_weight, out_weight, up_weight, down_weight, norm_gains, norm_biases, pre_weight, post_weight, codebook, quant_gain, quant_bias):
    qkv_low = low(qkv_weight)
    out_low = low(out_weight)
    up_low = low(up_weight)
    down_low = low(down_weight)
    gain_low = low(norm_gains)
    bias_low = low(norm_biases)
    pre_low = low(pre_weight)
    post_low = low(post_weight)
    qgain_low = low(quant_gain)
    qbias_low = low(quant_bias)
    code_vals = low(codebook)
    code_unit = code_vals * lax.rsqrt(lax.optimization_barrier(jnp.sum(code_vals * code_vals, axis=1, keepdims=True)) + 1.0)
    code_low = low(code_unit)
    weight = 1.0 / math.sqrt(TOKENS)

    def row_loss(total, inputs):
        row_vals, seg_row = inputs
        encoded = block(row_vals, seg_row, qkv_low[0], out_low[0], up_low[0], down_low[0], gain_low[0], bias_low[0])
        start_rows, commit = quantize(encoded, qgain_low, qbias_low, pre_low, post_low, code_low)
        decoded = block(start_rows, seg_row, qkv_low[1], out_low[1], up_low[1], down_low[1], gain_low[1], bias_low[1])
        error = decoded - row_vals
        return (total + weight * (0.5 * jnp.sum(error * error) + BETA * commit), None)
    total, unused = lax.scan(jax.checkpoint(row_loss), jnp.zeros((), jnp.float32), (tokens_f, segments))
    return total

def reference(tokens, segments, qkv_weight, out_weight, up_weight, down_weight, norm_gains, norm_biases, pre_weight, post_weight, codebook, quant_gain, quant_bias):
    primals = (tokens.astype(jnp.float32), qkv_weight, out_weight, up_weight, down_weight, norm_gains, norm_biases, pre_weight, post_weight, codebook, quant_gain, quant_bias)
    loss, pullback = jax.vjp(partial(forward, segments), *primals)
    grads = pullback(jnp.ones_like(loss))
    return (grads[0], grads[1], grads[2], grads[3], grads[4], grads[5], grads[6], grads[7], grads[8], grads[9], grads[10], grads[11])
```

```python
import math

import jax
import jax.numpy as jnp
from jax import lax
from jax.experimental import pallas as pl
from jax.experimental.pallas import tpu as pltpu
from jax.sharding import PartitionSpec as P

F32, BF16 = jnp.float32, jnp.bfloat16
VMEM = pltpu.VMEM
MESH = pl.DeviceIdType.MESH
HEADS = 8
HEAD_DIM = 64
EPS = 1e-05
BETA = 0.25
TEMP = 8.0
GELU_C = math.sqrt(2.0 / math.pi)
GELU_K = 0.044715
NEG_FILL = -1e30
LOG2E = math.log2(math.e)
D = 512
FF = 2048
CODES = 8192
CODE_DIM = 32
LENGTH = 512
GRID = (4, 2, 2)
SMALL, ATT, UP, DOWN, ROWS = 0, 32, 160, 288, 416
PARTS = ((SMALL, 160), (UP, 128), (DOWN, 128))
TT = 256
QT = 256
CB = 1024


def dot_nn(a, b):
    return jnp.dot(a, b, preferred_element_type=F32)


def dot_nt(a, b):
    return lax.dot_general(a, b, (((1,), (1,)), ((), ())), preferred_element_type=F32)


def dot_tn(a, b):
    return lax.dot_general(a, b, (((0,), (0,)), ((), ())), preferred_element_type=F32)


def norm_stats(x):
    center = jnp.mean(x, axis=-1, keepdims=True)
    shifted = x - center
    inv = lax.rsqrt(jnp.mean(shifted * shifted, axis=-1, keepdims=True) + EPS)
    return shifted * inv, inv


def norm_back(grad, normed, inv, gain):
    scaled = grad * gain
    return inv * (
        scaled
        - jnp.mean(scaled, axis=-1, keepdims=True)
        - normed * jnp.mean(scaled * normed, axis=-1, keepdims=True)
    )


def weight(w, j):
    return w[:, :, :, ATT + 32 * j : ATT + 32 * (j + 1), :].reshape(D, D)


def down_weight(w, f):
    return w[f, :, :, DOWN:ROWS, :].reshape(D, D)


def pair_lanes(hp, base=0):
    return pl.ds(pl.multiple_of(base + hp * 128, 128), 128)


def head_masks():
    lane = lax.broadcasted_iota(jnp.int32, (1, 128), 1)
    return (lane < HEAD_DIM).astype(F32).astype(BF16), (lane >= HEAD_DIM).astype(F32).astype(BF16)


def block_fwd(x_ref, w, vec, bias_ref, B, out_ref, pump):
    scale = LOG2E * HEAD_DIM**-0.5
    pump("att")
    for t in range(0, LENGTH, TT):
        rows = slice(t, t + TT)
        n, _ = norm_stats(x_ref[rows, :].astype(F32))
        a = (n * vec[0] + vec[1]).astype(BF16)
        B["attn_in"][rows, :] = a
        for j in range(3):
            B["qkv"][rows, j * D : (j + 1) * D] = dot_nn(a, weight(w, j)).astype(BF16)
        pump()
    B["vT"][...] = B["qkv"][:, 2 * D :].T
    masks = head_masks()

    def pair(hp, carry):
        q = B["qkv"][:, pair_lanes(hp)]
        k = B["qkv"][:, pair_lanes(hp, D)]
        for e in range(2):
            km = k * masks[e]
            h = hp * 2 + e
            hrows = pl.ds(pl.multiple_of(h * HEAD_DIM, HEAD_DIM), HEAD_DIM)
            vt = B["vT"][hrows, :]
            for c in range(0, LENGTH, QT):
                cols = slice(c, c + QT)
                s = dot_nt(km, q[cols, :]) * scale + bias_ref[:, cols]
                p = jnp.exp2(s - jnp.max(s, axis=0, keepdims=True))
                p = (p * (1.0 / jnp.sum(p, axis=0, keepdims=True))).astype(BF16)
                B["PT"][h, :, cols] = p
                B["mixT"][hrows, cols] = dot_nn(vt, p).astype(BF16)
        return carry

    for hp in range(0, HEADS // 2, 2):
        lax.fori_loop(hp, hp + 2, pair, 0)
        pump()
    pump("mlp")
    for t in range(0, LENGTH, TT):
        rows = slice(t, t + TT)
        mid = x_ref[rows, :].astype(F32) + dot_nn(B["mixT"][:, rows].T, weight(w, 3))
        B["mid"][rows, :] = mid
        n, _ = norm_stats(mid)
        a = (n * vec[2] + vec[3]).astype(BF16)
        B["mlp_in"][rows, :] = a
        acc = mid
        for f in range(4):
            u = dot_nn(a, weight(w, 4 + f))
            u2 = u * u
            th = jnp.tanh(u * (GELU_C + (GELU_C * GELU_K) * u2))
            half = 0.5 + 0.5 * th
            hid = (u * half).astype(BF16)
            slope = half + (0.5 * u) * (1.0 - th * th) * (GELU_C + (3.0 * GELU_C * GELU_K) * u2)
            fc = slice(f * D, (f + 1) * D)
            B["hid"][rows, fc] = hid
            B["slope"][rows, fc] = slope.astype(BF16)
            acc = acc + dot_nn(hid, down_weight(w, f))
        out_ref[rows, :] = acc
        pump()


def block_bwd(g_ref, x_ref, w, vec, B, put, pump):
    low = B["low"]
    sums = [jnp.zeros((1, D), F32) for _ in range(4)]
    low[...] = g_ref[...].astype(BF16)
    for f in range(4):
        fc = slice(f * D, (f + 1) * D)
        put.down(f, dot_tn(B["hid"][:, fc], low[...]))
    put.start("down")
    pump()
    for t in range(0, LENGTH, TT):
        rows = slice(t, t + TT)
        g = low[rows, :]
        acc = jnp.zeros((TT, D), F32)
        for f in range(4):
            fc = slice(f * D, (f + 1) * D)
            gp = (dot_nt(g, down_weight(w, f)) * B["slope"][rows, fc].astype(F32)).astype(BF16)
            B["slope"][rows, fc] = gp
            acc = acc + dot_nt(gp, weight(w, 4 + f))
        n, inv = norm_stats(B["mid"][rows, :])
        sums[2] = sums[2] + jnp.sum(acc * n, axis=0, keepdims=True)
        sums[3] = sums[3] + jnp.sum(acc, axis=0, keepdims=True)
        gm = g_ref[rows, :] + norm_back(acc, n, inv, vec[2])
        g_ref[rows, :] = gm
        gml = gm.astype(BF16)
        B["branch"][rows, :] = gml
        B["dmix"][rows, :] = dot_nt(gml, weight(w, 3)).astype(BF16)
        pump()
    m_t = B["mlp_in"][...].T
    for f in range(4):
        fc = slice(f * D, (f + 1) * D)
        put.up(f, dot_nn(m_t, B["slope"][:, fc]))
    put.start("up")
    put.att(3, dot_nn(B["mixT"][...], B["branch"][...]))
    pump()
    B["vT"][...] = B["qkv"][:, D : 2 * D].T
    masks = head_masks()

    def pair(hp, carry):
        q = B["qkv"][:, pair_lanes(hp)]
        v = B["qkv"][:, pair_lanes(hp, 2 * D)]
        dm = B["dmix"][:, pair_lanes(hp)]
        dv = jnp.zeros((LENGTH, 128), F32)
        dk = jnp.zeros((LENGTH, 128), F32)
        for e in range(2):
            vm = v * masks[e]
            h = hp * 2 + e
            hrows = pl.ds(pl.multiple_of(h * HEAD_DIM, HEAD_DIM), HEAD_DIM)
            kt = B["vT"][hrows, :]
            for c in range(0, LENGTH, QT):
                cols = slice(c, c + QT)
                p = B["PT"][h, :, cols].astype(F32)
                tt = p * dot_nt(vm, dm[cols, :])
                ds = (tt - p * jnp.sum(tt, axis=0, keepdims=True)).astype(BF16)
                B["ds"][:, cols] = ds
                B["mixT"][hrows, cols] = (dot_nn(kt, ds) * HEAD_DIM**-0.5).astype(BF16)
            dv = dv + dot_nn(B["PT"][h], dm * masks[e])
            dk = dk + dot_nn(B["ds"][...], q * masks[e])
        B["qkv"][:, pair_lanes(hp, D)] = (dk * HEAD_DIM**-0.5).astype(BF16)
        B["qkv"][:, pair_lanes(hp, 2 * D)] = dv.astype(BF16)
        return carry

    for hp in range(HEADS // 2):
        lax.fori_loop(hp, hp + 1, pair, 0)
        pump()
    B["qkv"][:, 0:D] = B["mixT"][...].T
    a_t = B["attn_in"][...].T
    for j in range(3):
        put.att(j, dot_nn(a_t, B["qkv"][:, j * D : (j + 1) * D]))
    for t in range(0, LENGTH, TT):
        rows = slice(t, t + TT)
        acc = dot_nt(B["qkv"][rows, 0:D], weight(w, 0))
        for j in range(1, 3):
            acc = acc + dot_nt(B["qkv"][rows, j * D : (j + 1) * D], weight(w, j))
        n, inv = norm_stats(x_ref[rows, :].astype(F32))
        sums[0] = sums[0] + jnp.sum(acc * n, axis=0, keepdims=True)
        sums[1] = sums[1] + jnp.sum(acc, axis=0, keepdims=True)
        g_ref[rows, :] = g_ref[rows, :] + norm_back(acc, n, inv, vec[0])
    return sums


def prepare_codes(w_ref, Q):
    for dev in range(32):
        sec, z, x, c = dev // 16, dev // 4 % 4, dev // 2 % 2, dev % 2
        v = w_ref[sec, z, x, c, 0:CODE_DIM, 0:256].astype(F32)
        low = (v * lax.rsqrt(jnp.sum(v * v, axis=0, keepdims=True) + 1.0)).astype(BF16)
        Q["codesT"][:, 256 * dev : 256 * dev + 256] = low
    for o in range(0, 2048, 512):
        four = [Q["codesT"][:, 2048 * g + o : 2048 * g + o + 512] for g in range(4)]
        Q["codes"][o : o + 512, :] = jnp.concatenate(four, axis=0).T


def place(Q, low, g):
    Q["group"][...] = jnp.zeros_like(Q["group"])
    Q["group"][32 * g : 32 * g + 32, :] = low


def quant_fwd(qv, pre_t, post, ET, Q, dec_ref, pump):
    for t in range(0, LENGTH, TT):
        rows = slice(t, t + TT)
        n, _ = norm_stats(Q["h"][rows, :])
        Q["mapped"][rows, :] = (n * qv[0] + qv[1]).astype(BF16)
    raw = dot_nt(pre_t, Q["mapped"][...])
    rescale = lax.rsqrt(jnp.sum(raw * raw, axis=0, keepdims=True) + 1.0)
    unit = raw * rescale
    Q["unit"][...] = unit
    Q["rescale"][...] = rescale
    low = unit.astype(BF16)

    def step(i, carry):
        acc, z = carry
        o = pl.multiple_of(i * CB, CB)
        here = pl.multiple_of(lax.rem(i, 2048 // CB) * CB, CB)
        logits = dot_nn(Q["codes"][pl.ds(here, CB), :], Q["group"][...])
        e = jnp.exp2(logits * (TEMP * LOG2E))
        z = z + jnp.sum(e, axis=0, keepdims=True)
        e = e.astype(BF16)
        ET[pl.ds(o, CB), :] = e
        return acc + dot_nn(Q["codesT"][:, pl.ds(o, CB)], e), z

    carry = (jnp.zeros((CODE_DIM, LENGTH), F32), jnp.zeros((1, LENGTH), F32))
    for i in range(0, CODES // CB, 2):
        place(Q, low, i // 2)
        carry = lax.fori_loop(i, i + 2, step, carry)
        pump()
    acc, z = carry
    rz = 1.0 / z
    mixture = acc * rz
    Q["rz"][...] = rz
    Q["mixture"][...] = mixture
    dec_ref[...] = dot_nn(mixture.astype(BF16).T, post).astype(BF16)


def quant_bwd(g_ref, qv, pre_t, post, ET, Q, low_ref, pull, gcodes, M, pump):
    low_ref[...] = g_ref[...].astype(BF16)
    mixture, unit, rz, rescale = Q["mixture"][...], Q["unit"][...], Q["rz"][...], Q["rescale"][...]
    qlow = mixture.astype(BF16)
    quant = qlow.astype(F32)
    M[32:64, :] = dot_nn(qlow, low_ref[...])
    gq = (dot_nt(post, low_ref[...]) + pull * (quant - unit)).astype(BF16)
    delta = jnp.sum(gq.astype(F32) * mixture, axis=0, keepdims=True)
    u8 = (unit.astype(BF16).astype(F32) * TEMP).astype(BF16)

    def step(i, acc):
        o = pl.multiple_of(i * CB, CB)
        here = pl.multiple_of(lax.rem(i, 2048 // CB) * CB, CB)
        p = ET[pl.ds(o, CB), :].astype(F32) * rz
        dp = dot_nn(Q["codes"][pl.ds(here, CB), :], Q["group"][...])
        dl = (p * (dp - delta)).astype(BF16)
        gcodes(i, dot_nt(gq, p.astype(BF16)) + dot_nt(u8, dl))
        return acc + dot_nn(Q["codesT"][:, pl.ds(o, CB)], dl)

    gu = jnp.zeros((CODE_DIM, LENGTH), F32)
    for i in range(0, CODES // CB, 2):
        place(Q, gq, i // 2)
        gu = lax.fori_loop(i, i + 2, step, gu)
        pump()
    gu = gu * TEMP + pull * (unit - quant)
    graw = (rescale * (gu - unit * jnp.sum(gu * unit, axis=0, keepdims=True))).astype(BF16)
    M[0:32, :] = dot_nn(graw, Q["mapped"][...])
    gr = graw.T
    sg = jnp.zeros((1, D), F32)
    sb = jnp.zeros((1, D), F32)
    for t in range(0, LENGTH, TT):
        rows = slice(t, t + TT)
        gm = dot_nn(gr[rows, :], pre_t)
        n, inv = norm_stats(Q["h"][rows, :])
        sg = sg + jnp.sum(gm * n, axis=0, keepdims=True)
        sb = sb + jnp.sum(gm, axis=0, keepdims=True)
        g_ref[rows, :] = norm_back(gm, n, inv, qv[0])
    M[64:65, :] = sg
    M[65:66, :] = sb


def picks():
    row = lax.broadcasted_iota(jnp.int32, (D, 256), 0)
    col = lax.broadcasted_iota(jnp.int32, (D, 256), 1)
    at = col + (col - lax.rem(col, 16))
    return tuple((row == at + 16 * k).astype(F32).astype(BF16) for k in range(2))


def unpack_small(w_ref, small_t):
    small_t[...] = w_ref[:, :, :, :, 0:16, 256:384].reshape(D, 128).T
    lo, hi = picks()
    vecs = []
    for sec in range(2):
        cols = slice(256 * sec, 256 * sec + 256)
        part = small_t[64:80, cols]
        full = dot_nt(part, lo)
        other = dot_nt(part, hi)
        vecs.append([full[2 + i : 3 + i, :] + other[6 + i : 7 + i, :] for i in range(4)])
    qv = small_t[64:66, :].astype(F32)
    return vecs, (qv[0:1, :], qv[1:2, :])


def pack_norms(M, sec, sums):
    lo, hi = picks()
    rows = jnp.concatenate(sums + [jnp.zeros((4, D), F32)], axis=0).astype(BF16)
    cols = slice(256 * sec, 256 * sec + 256)
    M[66:70, cols] = dot_nn(rows, lo)[0:4, :]
    M[70:74, cols] = dot_nn(rows, hi)[0:4, :]


def remote(src, dst, send_sem, recv_sem, device):
    return pltpu.make_async_remote_copy(
        src_ref=src, dst_ref=dst, send_sem=send_sem, recv_sem=recv_sem, device_id=device, device_id_type=MESH
    )


class Place:
    def __init__(self):
        self.s = lax.axis_index("section")
        dp = lax.axis_index("dp")
        self.z, self.x, self.c = lax.div(dp, 4), lax.rem(lax.div(dp, 2), 2), lax.rem(dp, 2)
        self.zu, self.zd, self.zo = lax.rem(self.z + 1, 4), lax.rem(self.z + 3, 4), lax.rem(self.z + 2, 4)
        self.up = (self.s, self.zu * 4 + self.x * 2 + self.c)
        self.dn = (self.s, self.zd * 4 + self.x * 2 + self.c)
        self.xp = (self.s, self.z * 4 + (1 - self.x) * 2 + self.c)
        self.cp = (self.s, self.z * 4 + self.x * 2 + (1 - self.c))
        self.yp = (1 - self.s, dp)

    def neighbours(self):
        return (self.up, self.dn, self.xp, self.cp, self.yp)


class Gather:
    def __init__(self, me, w, send_sem, recv_sem):
        self.me, self.w, self.ss, self.rs = me, w, send_sem, recv_sem
        self.sent = []
        self.list = [(sec, part) for sec in range(2) for part in range(3)]
        self.order = self.steps()
        self.done = -1

    def at(self, k, z, x, c):
        sec, part = self.list[k]
        lo, n = PARTS[part]
        return self.w.at[sec, z, x, c, pl.ds(lo, n), :]

    def move(self, k, kind, ref, device):
        copy = remote(ref, ref, self.ss.at[k, kind], self.rs.at[k, kind], device)
        copy.start()
        self.sent.append((None, copy))

    def land(self, k, kind, ref):
        remote(ref, ref, self.ss.at[k, kind], self.rs.at[k, kind], self.me.yp).wait_recv()

    def begin(self):
        me = self.me
        for k, (sec, _) in enumerate(self.list):
            ref = self.at(k, me.z, me.x, me.c)
            copy = remote(ref, ref, self.ss.at[k, 0], self.rs.at[k, 0], me.yp)
            pl.when(me.s == sec)(copy.start)
            self.sent.append((sec, copy))

    def over_x(self, k):
        me, (sec, _) = self.me, self.list[k]
        ref = self.at(k, me.z, me.x, me.c)
        pl.when(me.s != sec)(lambda: self.land(k, 0, ref))
        self.move(k, 1, ref, me.xp)

    def over_z(self, k):
        me = self.me
        self.land(k, 1, self.at(k, me.z, 1 - me.x, me.c))
        ref = self.at(k, me.z, slice(None), me.c)
        self.move(k, 2, ref, me.up)
        self.move(k, 3, ref, me.dn)

    def onward(self, k):
        me = self.me
        self.land(k, 2, self.at(k, me.zd, slice(None), me.c))
        self.move(k, 4, self.at(k, me.zd, 0, me.c), me.up)
        self.land(k, 3, self.at(k, me.zu, slice(None), me.c))
        self.move(k, 5, self.at(k, me.zu, 1, me.c), me.dn)

    def over_core(self, k):
        me = self.me
        self.land(k, 4, self.at(k, me.zo, 0, me.c))
        self.land(k, 5, self.at(k, me.zo, 1, me.c))
        self.move(k, 6, self.at(k, slice(None), slice(None), me.c), me.cp)

    def ready(self, k):
        self.land(k, 6, self.at(k, slice(None), slice(None), 1 - self.me.c))
        self.done = k

    def steps(self):
        stages = (self.over_x, self.over_z, self.onward, self.over_core, self.ready)
        for t in range(len(self.list) + len(stages)):
            for i, stage in reversed(list(enumerate(stages))):
                if 0 <= t - i < len(self.list):
                    yield stage(t - i)

    def pump(self):
        next(self.order, None)

    def need(self, k):
        while self.done < k:
            next(self.order)

    def finish(self):
        for _ in self.order:
            pass
        for sec, copy in self.sent:
            if sec is None:
                copy.wait_send()
            else:
                pl.when(self.me.s == sec)(copy.wait_send)


class Reduce:
    def __init__(self, me, G, land, work, send_sem, recv_sem, free_sem, outs, finish_codes):
        self.finish_codes = finish_codes
        self.me, self.G, self.land, self.work = me, G, land, work
        self.ss, self.rs, self.free, self.outs = send_sem, recv_sem, free_sem, outs
        self.live = []
        self.open = {}

    def copies(self, k, kind):
        me, G, L, W = self.me, self.G[k], self.land[k], self.work[k]
        src, dst, device = {
            0: lambda: (G.at[:, :, 1 - me.c], L["core"], me.cp),
            1: lambda: (G.at[me.zo, 0, me.c], L["z1"].at[0], me.up),
            2: lambda: (G.at[me.zo, 1, me.c], L["z1"].at[1], me.dn),
            3: lambda: (G.at[me.zu, :, me.c], L["z2"].at[0], me.up),
            4: lambda: (G.at[me.zd, :, me.c], L["z2"].at[1], me.dn),
            5: lambda: (W["out"], L["x"], me.xp),
            6: lambda: (W["out"], L["y"], me.yp),
        }[kind]()
        return remote(src, dst, self.ss.at[k, kind], self.rs.at[k, kind], device)

    def go(self, k, kind):
        self.copies(k, kind).start()

    def settle(self, k):
        self.complete(k)
        for sec in self.open.pop(k, ()):
            for kind in range(5):
                self.copies(k, kind).wait_send()
            pl.when(self.me.s != sec)(self.copies(k, 6).wait_send)

    def complete(self, k):
        while any(part == k for part, _ in self.live):
            self.pump()

    def start(self, k, sec):
        self.complete(k)
        if sec == 0:
            pl.semaphore_wait(self.free.at[k], 5)
        self.go(k, 0)
        self.open[k] = (sec,)
        self.live.append((k, self.run(k, sec)))

    def run(self, k, sec):
        me, G, L, W = self.me, self.G[k], self.land[k], self.work[k]
        f = lambda v: v.astype(F32)
        self.copies(k, 0).wait_recv()
        for z in range(4):
            G[z, :, me.c] = (f(G[z, :, me.c]) + f(L["core"][z])).astype(BF16)
        self.go(k, 1)
        self.go(k, 2)
        yield
        self.copies(k, 1).wait_recv()
        G[me.zu, 0, me.c] = (f(G[me.zu, 0, me.c]) + f(L["z1"][0])).astype(BF16)
        self.go(k, 3)
        self.copies(k, 2).wait_recv()
        G[me.zd, 1, me.c] = (f(G[me.zd, 1, me.c]) + f(L["z1"][1])).astype(BF16)
        self.go(k, 4)
        yield
        self.copies(k, 3).wait_recv()
        self.copies(k, 4).wait_recv()
        total = lambda x: f(G[me.z, x, me.c]) + f(L["z2"][0, x]) + f(L["z2"][1, x])
        W["out"][...] = total(1 - me.x).astype(BF16)
        self.go(k, 5)
        if sec == 0:
            pl.when(me.s == 1)(lambda: [copy.wait() for copy in self.outs(k)] and None)
        W["acc"][...] = total(me.x)
        yield
        self.copies(k, 5).wait_recv()
        W["acc"][...] += f(L["x"][...])

        self.copies(k, 5).wait_send()

        @pl.when(me.s != sec)
        def _():
            W["out"][...] = W["acc"][...].astype(BF16)
            self.copies(k, 6).start()

        yield

        @pl.when(me.s == sec)
        def _():
            self.copies(k, 6).wait_recv()
            W["acc"][...] += f(L["y"][...])
            self.finish_codes(k)
            for copy in self.outs(k):
                copy.start()

        if sec == 1:
            for device in me.neighbours():
                pl.semaphore_signal(self.free.at[k], inc=1, device_id=device, device_id_type=MESH)

    def pump(self):
        for item in list(self.live):
            try:
                next(item[1])
            except StopIteration:
                self.live.remove(item)

    def finish(self):
        while self.live:
            self.pump()
        for k in list(self.open):
            self.settle(k)
            pl.when(self.me.s == 0)(lambda: [copy.wait() for copy in self.outs(k)] and None)


class Put:
    def __init__(self, reduce, sec):
        self.reduce, self.sec = reduce, sec
        self.fresh = set()

    def buffer(self, k):
        if k not in self.fresh:
            self.fresh.add(k)
            self.reduce.settle(k)
        return self.reduce.G[k]

    def down(self, f, value):
        self.buffer(0)[f] = value.astype(BF16).reshape(2, 2, 128, D)

    def up(self, f, value):
        self.buffer(1)[:, :, :, 32 * f : 32 * f + 32, :] = value.astype(BF16).reshape(GRID + (32, D))

    def att(self, j, value):
        self.buffer(2)[:, :, :, 32 * (j + 1) : 32 * (j + 2), :] = value.astype(BF16).reshape(GRID + (32, D))

    def start(self, name):
        self.reduce.start({"down": 0, "up": 1, "att": 2}[name], self.sec)


class PutHbm:
    def __init__(self, g, slots, sems, sec):
        self.g, self.slots, self.sems, self.sec = g, slots, sems, sec

    def down(self, f, value):
        self.slots[0][...] = value.astype(BF16).reshape(2, 2, 128, D)
        pltpu.make_async_copy(self.slots[0], self.g.at[self.sec, f, :, :, pl.ds(DOWN, 128), :], self.sems.at[0]).start()
        pltpu.make_async_copy(self.slots[0], self.g.at[self.sec, f, :, :, pl.ds(DOWN, 128), :], self.sems.at[0]).wait()

    def rows(self, j, value):
        self.slots[1][...] = value.astype(BF16).reshape(GRID + (32, D))
        copy = pltpu.make_async_copy(self.slots[1], self.g.at[self.sec, :, :, :, pl.ds(32 * j, 32), :], self.sems.at[1])
        copy.start()
        copy.wait()

    def up(self, f, value):
        self.rows(f + 5, value)

    def att(self, j, value):
        self.rows(j + 1, value)

    def start(self, name):
        pass


BLOCK = dict(
    attn_in=((LENGTH, D), BF16),
    qkv=((LENGTH, 3 * D), BF16),
    PT=((HEADS, LENGTH, LENGTH), BF16),
    mixT=((D, LENGTH), BF16),
    mid=((LENGTH, D), F32),
    mlp_in=((LENGTH, D), BF16),
    hid=((LENGTH, FF), BF16),
    slope=((LENGTH, FF), BF16),
)
SHARED = dict(
    vT=((D, LENGTH), BF16),
    ds=((LENGTH, LENGTH), BF16),
    low=((LENGTH, D), BF16),
    branch=((LENGTH, D), BF16),
    dmix=((LENGTH, D), BF16),
)
QUANT = dict(
    mapped=((LENGTH, D), BF16),
    unit=((CODE_DIM, LENGTH), F32),
    rescale=((1, LENGTH), F32),
    rz=((1, LENGTH), F32),
    mixture=((CODE_DIM, LENGTH), F32),
    h=((LENGTH, D), F32),
    codesT=((CODE_DIM, CODES), BF16),
    codes=((2048, 128), BF16),
    group=((128, LENGTH), BF16),
)
STATE = dict(
    x=((LENGTH, D), BF16),
    bias=((LENGTH, LENGTH), F32),
    dec=((LENGTH, D), BF16),
    fx=((LENGTH, D), F32),
    ET=((CODES, LENGTH), BF16),
    M=((128, D), F32),
    smallT=((128, D), BF16),
    GS=((2,) + GRID + (32, 384), BF16),
)
GROUPS = (BLOCK, SHARED, QUANT, STATE)
KEPT = tuple(BLOCK) + ("top",)


def kept_shapes():
    return [jax.ShapeDtypeStruct(*BLOCK[k]) for k in BLOCK] + [jax.ShapeDtypeStruct((LENGTH, D), F32)]


def group_scratch():
    return [VMEM(*shape) for group in GROUPS for shape in group.values()]


def split_groups(refs):
    refs = iter(refs)
    return [{k: next(refs) for k in group} for group in GROUPS]


def row_program(w, seg_row, wt, S, kept, kept_sem, steps, put_of, small_done):
    block, shared, Q, T = S
    B = {**block, **shared}
    seg_col = jnp.broadcast_to(seg_row.astype(F32), (8, LENGTH)).T[:, 0:1]
    T["bias"][...] = jnp.where(seg_col == seg_row.astype(F32), 0.0, NEG_FILL)
    T["M"][...] = jnp.zeros_like(T["M"])
    T["GS"][...] = jnp.zeros_like(T["GS"])

    def pump_for(sec):
        def pump(name=None):
            if name is None:
                steps.pump()
            else:
                steps.need(3 * sec + (0 if name == "att" else 2))

        return pump

    steps.need(0)
    small = w.at[0]
    steps.need(3)
    vecs, qv = unpack_small(w, T["smallT"])
    prepare_codes(w, Q)
    pre_t, post = T["smallT"][0:32, :], T["smallT"][32:64, :]
    block_fwd(T["x"], w.at[0], vecs[0], T["bias"], B, Q["h"], pump_for(0))
    outs = [pltpu.make_async_copy(B[k], h, kept_sem.at[i]) for i, (k, h) in enumerate(zip(BLOCK, kept))]
    for copy in outs:
        copy.start()
    quant_fwd(qv, pre_t, post, T["ET"], Q, T["dec"], steps.pump)
    for copy in outs:
        copy.wait()
    block_fwd(T["dec"], w.at[1], vecs[1], T["bias"], B, T["fx"], pump_for(1))
    steps.gathered()
    T["fx"][...] = (T["fx"][...] - T["x"][...].astype(F32)) * wt
    top = pltpu.make_async_copy(T["fx"], kept[-1], kept_sem.at[len(BLOCK)])
    top.start()
    top.wait()
    put = put_of(1)
    sums = block_bwd(T["fx"], T["dec"], w.at[1], vecs[1], B, put, steps.pump)
    pack_norms(T["M"], 1, sums)
    ins = [pltpu.make_async_copy(h, B[k], kept_sem.at[i]) for i, (k, h) in enumerate(zip(BLOCK, kept))]
    for copy in ins:
        copy.start()

    def gcodes(i, value):
        for m in range(4):
            T["GS"][lax.div(i, 4), lax.rem(i, 4), m // 2, m % 2, :, 0:256] = value[:, 256 * m : 256 * m + 256].astype(BF16)

    quant_bwd(T["fx"], qv, pre_t, post, T["ET"], Q, B["low"], 2.0 * BETA * wt, gcodes, T["M"], steps.pump)
    for copy in ins:
        copy.wait()
    back = pltpu.make_async_copy(kept[-1], Q["h"], kept_sem.at[len(BLOCK)])
    back.start()
    small_done(1, T)
    put.start("att")
    put = put_of(0)
    sums = block_bwd(T["fx"], T["x"], w.at[0], vecs[0], B, put, steps.pump)
    pack_norms(T["M"], 0, sums)
    small_done(0, T)
    put.start("att")
    back.wait()


def small_rows(T, sec):
    T["GS"][sec, :, :, :, 0:16, 256:384] = (
        T["M"][:, 256 * sec : 256 * sec + 256].T.astype(BF16).reshape(GRID + (16, 128))
    )


def fused_kernel(wt, *refs):
    tokens, segments, w_qkv, w_out, w_up, w_down, small, codes_t = refs[:8]
    g_tok, g_qkv, g_out, g_up, g_down, g_small, g_codes = refs[8:15]
    nk = len(KEPT)
    kept = refs[15 : 15 + nk]
    refs = refs[15 + nk :]
    w, swap_land, done_codes = refs[:3]
    G, lands, works = refs[3:6], refs[6:21], refs[21:27]
    kept_sem, gs, gr, rs, rr, free, ts, out_sem, in_sem = refs[27:36]
    S = split_groups(refs[36:])
    block, shared, Q, T = S
    me = Place()
    own = w.at[me.s, me.z, me.x, me.c]
    half = LENGTH // 2
    mine = T["x"].at[pl.ds(pl.multiple_of(me.s * half, half), half), :]
    theirs = T["x"].at[pl.ds(pl.multiple_of((1 - me.s) * half, half), half), :]
    pieces = [(w_qkv.at[:, pl.ds(D * q, D)], 32 * q, 32) for q in range(3)] + [(w_out, 96, 32)]
    pieces += [(w_up.at[:, pl.ds(D * q, D)], 128 + 32 * q, 32) for q in range(4)] + [(w_down, 256, 128)]
    loads = [
        pltpu.make_async_copy(src, T["fx"].at[pl.ds(lo, n), :], in_sem.at[i]) for i, (src, lo, n) in enumerate(pieces)
    ]
    loads.append(pltpu.make_async_copy(tokens.at[me.s], mine, in_sem.at[len(pieces)]))
    for copy in loads:
        copy.start()
    own[0:32, 0:256] = codes_t[...].astype(BF16)
    own[0:16, 256:384] = small[...].astype(BF16)
    for copy in loads:
        copy.wait()
    own[ATT:ROWS, :] = T["fx"][0 : ROWS - ATT, :].astype(BF16)
    barrier = pltpu.get_barrier_semaphore()
    for device in me.neighbours():
        pl.semaphore_signal(barrier, inc=1, device_id=device, device_id_type=MESH)
    pl.semaphore_wait(barrier, 5)

    gather = Gather(me, w, gs, gr)
    gather.begin()
    give = remote(tokens.at[1 - me.s], mine, ts.at[0], ts.at[1], me.yp)
    give.start()

    def outs(k):
        acc = work[k]["acc"]
        if k == 0:
            pairs = [(acc, g_down)]
        elif k == 1:
            pairs = [(acc.at[pl.ds(32 * f, 32), :], g_up.at[:, pl.ds(D * f, D)]) for f in range(4)]
        else:
            pairs = [(acc.at[pl.ds(32 * (j + 1), 32), :], g_qkv.at[:, pl.ds(D * j, D)]) for j in range(3)]
            pairs += [(acc.at[pl.ds(128, 32), :], g_out), (acc.at[pl.ds(0, 16), pl.ds(256, 128)], g_small)]
            pairs += [(done_codes, g_codes)]
        return [pltpu.make_async_copy(src, dst, out_sem.at[k, i]) for i, (src, dst) in enumerate(pairs)]

    def finish_codes(k):
        if k == 2:
            ug = work[k]["acc"][0:32, 0:256]
            cv = own[0:32, 0:256].astype(F32)
            scale = lax.rsqrt(jnp.sum(cv * cv, axis=0, keepdims=True) + 1.0)
            unit = cv * scale
            done_codes[...] = scale * (ug - unit * jnp.sum(ug * unit, axis=0, keepdims=True))

    land = [dict(zip(("core", "z1", "z2", "x", "y"), lands[5 * k : 5 * k + 5])) for k in range(3)]
    work = [dict(zip(("out", "acc"), works[2 * k : 2 * k + 2])) for k in range(3)]
    reduce = Reduce(me, G, land, work, rs, rr, free, outs, finish_codes)

    class Steps:
        def __init__(self):
            self.first = True

        def need(self, k):
            if self.first:
                remote(theirs, theirs, ts.at[0], ts.at[1], me.yp).wait_recv()
                self.first = False
            gather.need(k)

        def pump(self):
            gather.pump()
            reduce.pump()

        def gathered(self):
            gather.finish()

    puts = {}

    def put_of(sec):
        puts[sec] = Put(reduce, sec)
        return puts[sec]

    def small_done(sec, T):
        small_rows(T, sec)
        puts[sec].buffer(2)[:, :, :, 0:32, 0:384] = T["GS"][sec]

    row_program(w, segments[pl.ds(me.s, 1), :], wt, S, kept, kept_sem, Steps(), put_of, small_done)
    here = pl.ds(pl.multiple_of(me.s * half, half), half)
    there = pl.ds(pl.multiple_of((1 - me.s) * half, half), half)
    T["fx"][...] = T["fx"][...] - Q["h"][...]
    swap = shared["low"].at[0:half, :]
    swap[...] = T["fx"][there, :].astype(BF16)
    send = remote(swap, swap_land, ts.at[2], ts.at[3], me.yp)
    send.start()
    keep = pltpu.make_async_copy(T["fx"].at[here, :], g_tok.at[me.s], ts.at[4])
    keep.start()
    give.wait_send()
    send.wait_recv()
    Q["h"][0:half, :] = swap_land[...].astype(F32)
    other = pltpu.make_async_copy(Q["h"].at[0:half, :], g_tok.at[1 - me.s], ts.at[5])
    other.start()
    reduce.finish()
    for k in range(3):
        pl.semaphore_wait(free.at[k], 0) if False else None
    send.wait_send()
    keep.wait()
    other.wait()


def plain_kernel(wt, *refs):
    x, segments, w_hbm = refs[:3]
    g_tok, g_w, g_small = refs[3:6]
    nk = len(KEPT)
    kept = refs[6 : 6 + nk]
    w, slot0, slot1, kept_sem, sems = refs[6 + nk : 11 + nk]
    S = split_groups(refs[11 + nk :])
    block, shared, Q, T = S
    load = pltpu.make_async_copy(w_hbm, w, sems.at[2])
    load.start()
    load.wait()
    T["x"][...] = x[...]

    class Steps:
        def need(self, k):
            pass

        def pump(self):
            pass

        def gathered(self):
            pass

    def small_done(sec, T):
        small_rows(T, sec)
        g_small[sec] = T["GS"][sec]

    put_of = lambda sec: PutHbm(g_w, (slot0, slot1), sems, sec)
    row_program(w, segments[...], wt, S, kept, kept_sem, Steps(), put_of, small_done)
    g_tok[...] = T["fx"][...] - Q["h"][...]


def pack_small(pre, post, qgain, qbias, gains, biases):
    n = pre.shape[0]
    cols = [pre, jnp.transpose(post, (1, 2, 0)), qgain[..., None], qbias[..., None]]
    both = jnp.stack([gains, biases], axis=2).reshape(n, 4, 2, 16)
    cols.append(jnp.transpose(both, (0, 3, 2, 1)).reshape(n, 16, 8))
    cols.append(jnp.zeros((n, 16, 128 - 74), F32))
    return jnp.concatenate(cols, axis=2)


def unpack_grads(small):
    n = small.shape[0]
    both = jnp.transpose(small[:, :, 66:74].reshape(n, 16, 2, 4), (0, 3, 2, 1)).reshape(n, 2, 2, 32)
    return (
        small[:, :, 0:32],
        jnp.transpose(small[:, :, 32:64], (0, 2, 1)),
        small[:, :, 64],
        small[:, :, 65],
        both[:, :, 0],
        both[:, :, 1],
    )


V = pl.BlockSpec(memory_space=VMEM)
H = pl.BlockSpec(memory_space=pl.ANY)
LIMIT = 64 * 1024 * 1024 - 256 * 1024


def fused_device(wt, tokens, segments, w_qkv, w_out, w_up, w_down, gains, biases, pre, post, codes, qgain, qbias):
    small = pack_small(pre[None], post[:, None], qgain[None], qbias[None], gains, biases)[0]
    shape = lambda *a, dtype=F32: jax.ShapeDtypeStruct(a, dtype)
    dma = pltpu.SemaphoreType.DMA
    rows = (128, 128, 160)
    parts = [VMEM(GRID + (n, D), BF16) for n in rows]
    lands = [
        VMEM(lead + (n, D), BF16) for n in rows for lead in ((4, 2), (2,), (2, 2), (), ())
    ]
    works = [VMEM((n, D), t) for n in rows for t in (BF16, F32)]
    outs = pl.pallas_call(
        lambda *refs: fused_kernel(wt, *refs),
        name="rows_and_exchange",
        out_shape=[
            shape(2, LENGTH // 2, D),
            shape(32, 3 * D),
            shape(32, D),
            shape(32, FF),
            shape(128, D),
            shape(16, 128),
            shape(CODE_DIM, 256),
        ]
        + kept_shapes(),
        in_specs=[H, V] + [H] * 4 + [V] * 2,
        out_specs=[H] * (7 + len(KEPT)),
        scratch_shapes=[VMEM((2,) + GRID + (ROWS, D), BF16), VMEM((LENGTH // 2, D), BF16), VMEM((CODE_DIM, 256), F32)]
        + parts
        + lands
        + works
        + [dma((len(KEPT),)), dma((6, 7)), dma((6, 7)), dma((3, 7)), dma((3, 7)), pltpu.SemaphoreType.REGULAR((3,)), dma((6,)), dma((3, 6)), dma((10,))]
        + group_scratch(),
        compiler_params=pltpu.CompilerParams(collective_id=0, has_side_effects=True, vmem_limit_bytes=LIMIT),
    )(tokens, segments, w_qkv[0], w_out[0], w_up[0], w_down[0], small, codes.T)
    g_tok, g_qkv, g_out, g_up, g_down, g_small, g_codes = outs[:7]
    g_pre, g_post, g_qg, g_qb, g_gains, g_biases = unpack_grads(g_small[None])
    return (
        g_tok, g_qkv[None], g_out[None], g_up[None], g_down[None], g_gains, g_biases,
        g_pre[0], g_post[0], g_codes.T, g_qg[0], g_qb[0],
    )


def plain_device(wt, tokens, segments, w_qkv, w_out, w_up, w_down, gains, biases, pre, post, codes, qgain, qbias):
    every = ("section", "dp")
    sec = lax.axis_index("section")
    low = lambda v: v.astype(BF16)
    both = lambda v, axis: lax.all_gather(lax.all_gather(low(v), "dp", axis=axis, tiled=True), "section", axis=0, tiled=True)
    x = lax.all_to_all(tokens, "section", 0, 1, tiled=True)[0]
    seg = lax.dynamic_slice_in_dim(segments, sec, 1, 0)
    qkv, out, up, down = (both(v, 1) for v in (w_qkv, w_out, w_up, w_down))
    gain, bias = both(gains, 2), both(biases, 2)
    pre, codes, qgain, qbias = (lax.all_gather(low(v), every, axis=0, tiled=True) for v in (pre, codes, qgain, qbias))
    post = lax.all_gather(low(post), every, axis=1, tiled=True)
    norms = lambda v: jnp.transpose(v.reshape(2, 2, 16, 32), (0, 2, 1, 3)).reshape(32, 2, 32)
    small = pack_small(
        *(v.astype(F32) for v in (pre.reshape(32, 16, 32), post.reshape(32, 32, 16), qgain.reshape(32, 16), qbias.reshape(32, 16))),
        norms(gain).astype(F32), norms(bias).astype(F32),
    )
    head = jnp.concatenate(
        [
            jnp.transpose(codes.reshape(32, 256, 32), (0, 2, 1)),
            jnp.pad(low(small), ((0, 0), (0, 16), (0, 0))),
            jnp.zeros((32, 32, 128), BF16),
        ],
        axis=2,
    ).reshape(2, 16, 32, D)
    cut = lambda v: jnp.transpose(v.reshape(2, 16, 32, -1, D), (0, 1, 3, 2, 4)).reshape(2, 16, -1, D)
    w = jnp.concatenate([head, cut(qkv), cut(out), cut(up), down.reshape(2, 16, 128, D)], axis=2)
    shape = lambda a, dtype=F32: jax.ShapeDtypeStruct(a, dtype)
    dma = pltpu.SemaphoreType.DMA
    full = (2,) + GRID + (ROWS, D)
    outs = pl.pallas_call(
        lambda *refs: plain_kernel(wt, *refs),
        name="rows",
        out_shape=[shape((LENGTH, D)), shape(full, BF16), shape((2,) + GRID + (32, 384), BF16)] + kept_shapes(),
        in_specs=[V, V, H],
        out_specs=[V, H, V] + [H] * len(KEPT),
        scratch_shapes=[VMEM(full, BF16), VMEM((2, 2, 128, D), BF16), VMEM(GRID + (32, D), BF16), dma((len(KEPT),)), dma((3,))]
        + group_scratch(),
        compiler_params=pltpu.CompilerParams(vmem_limit_bytes=LIMIT),
    )(x, seg, w.reshape(full))
    g_tok, g_w, g_small = outs[:3]
    g_tok = lax.all_to_all(low(g_tok)[None], "section", 1, 0, tiled=True).astype(F32)
    g_w = g_w.reshape(2, 16, ROWS, D)
    g_small = g_small.reshape(32, 32, 384)
    sum_dp = lambda v, axis: lax.psum_scatter(lax.psum_scatter(v, "section", scatter_dimension=0, tiled=True), "dp", scatter_dimension=axis, tiled=True)
    uncut = lambda lo, n: jnp.transpose(g_w[:, :, lo : lo + 32 * n].reshape(2, 16, n, 32, D), (0, 1, 3, 2, 4)).reshape(2, D, n * D).astype(F32)
    sums = [sum_dp(v, 1) for v in (uncut(ATT, 3), uncut(ATT + 96, 1), uncut(UP, 4), g_w[:, :, DOWN:].reshape(2, FF, D).astype(F32))]
    g_pre, g_post, g_qg, g_qb, g_gains, g_biases = unpack_grads(g_small[:, 0:16, 256:384].astype(F32))
    norms = lambda v: sum_dp(jnp.transpose(v.reshape(2, 16, 2, 32), (0, 2, 1, 3)).reshape(2, 2, D), 2)
    scatter = lambda v, axis=0: lax.psum_scatter(v, every, scatter_dimension=axis, tiled=True)
    ug = jnp.transpose(g_small[:, :, 0:256], (0, 2, 1)).reshape(CODES, CODE_DIM).astype(F32)
    cv = codes.astype(F32)
    scale = lax.rsqrt(jnp.sum(cv * cv, axis=1, keepdims=True) + 1.0)
    unit = cv * scale
    g_codes = scale * (ug - unit * jnp.sum(ug * unit, axis=1, keepdims=True))
    return (
        g_tok, *sums, norms(g_gains), norms(g_biases),
        scatter(g_pre.reshape(D, 32)), scatter(jnp.transpose(g_post, (1, 0, 2)).reshape(32, D), 1),
        scatter(g_codes), scatter(g_qg.reshape(D)), scatter(g_qb.reshape(D)),
    )


def solution(mesh):
    fused = mesh.shape["section"] == 2 and mesh.shape["dp"] == 16
    wt = 1.0 / math.sqrt(2 * mesh.shape["dp"] * LENGTH)
    device = fused_device if fused else plain_device
    split, rows = P("section", "dp", None), P(("section", "dp"), None)
    norms, vector = P("section", None, "dp"), P(("section", "dp"))
    columns = P(None, ("section", "dp"))
    shards = (split, split, split, split, norms, norms, rows, columns, rows, vector, vector)
    return jax.shard_map(
        lambda *args: device(wt, *args),
        mesh=mesh,
        in_specs=(P("dp", "section", None), P("dp", None)) + shards,
        out_specs=(P("dp", "section", None),) + shards,
        check_vma=False,
    )
```
